128 devices in a mesh: dp: 4 (over y), ep: 32 (over x, z, core).
Axes of the slice: x: 4, y: 4, z: 4, core: 2. Of those that a mesh axis runs over, the one named last changes fastest.
Arguments:
- query_plain: bfloat16 [4, 512, 8192], P(None, 'dp', 'ep'), may hold values from -6 to 6
- query_rotary: bfloat16 [4, 512, 4096], P(None, 'dp', 'ep'), may hold values from -6 to 6
- key_up: bfloat16 [64, 128, 512], P('ep'), may hold values from -0.5 to 0.5
- value_up: bfloat16 [64, 512, 128], P('ep'), may hold values from -0.25 to 0.25
- output_weight: bfloat16 [8192, 3584], P('ep'), may hold values from -0.0625 to 0.0625
- cache_latent: bfloat16 [512, 64, 512], P(('dp', 'ep')), may hold values from -6 to 6
- cache_rotary: bfloat16 [512, 64, 64], P(('dp', 'ep')), may hold values from -18 to 18
- lengths: int32 [512], P(('dp', 'ep')), may hold values from 2 to 64, as said below
- new_latent: bfloat16 [4, 512, 512], P(None, ('dp', 'ep')), may hold values from -6 to 6
- new_rotary: bfloat16 [4, 512, 64], P(None, ('dp', 'ep')), may hold values from -6 to 6
- residual: bfloat16 [4, 512, 3584], P(None, ('dp', 'ep')), may hold values from -1.5 to 1.5
- norm_gain: float32 [3584], replicated, may hold values from 0.5 to 1.5
- expert_ids: int32 [4, 512, 8], P(None, ('dp', 'ep')), may hold values from 0 to 127, all different within a row; in each aligned block of 4 rows (0 to 3, 4 to 7, ..., all dimensions but the last counted through in order) at most 2 rows name the same one
- gate_weights: float32 [4, 512, 8], P(None, ('dp', 'ep')), may hold values from 0.05 to 0.5
- expert_gate: bfloat16 [128, 3584, 1024], P(('dp', 'ep')), may hold values from -0.09375 to 0.09375
- expert_up: bfloat16 [128, 3584, 1024], P(('dp', 'ep')), may hold values from -0.09375 to 0.09375
- expert_down: bfloat16 [128, 1024, 3584], P(('dp', 'ep')), may hold values from -0.1875 to 0.1875
Outputs:
- layer_out: bfloat16 [4, 512, 3584], P(None, ('dp', 'ep'))
The draws below stay inside these ranges and needn't reach their ends.
Inputs may be any that keep to these rules, and one draw needn't show every extreme that they name: `expert_ids`: in each aligned block of 4 rows of one step no expert is named by more than 2 rows, a bound that some block reaches. `lengths`: some row has exactly 64 live positions.
All inputs are finite; a program needn't handle non-finite values.
Results may differ from the reference program's by a relative error of at most 0.025.
Values may be sent and summed in bfloat16 or wider, within the bound.
No kernel may reach another device: no remote copies, remote signals or barrier semaphores. Data moves between devices by JAX's collectives and lax.ppermute only.
A program may use at most 128 MiB of HBM per device.

```python
import math
import jax
import jax.numpy as jnp
import numpy as np
from jax import lax

D = 3584
HID = 1024
HEADS = 64
LAT = 512
ROPE = 64
NOPE = 128
VHEAD = 128
TOP = 8
MOST = 2
STEPS = 4
EXPERTS = 128
ROWS_DEV = 4
LMAX = 64
ROWS = 512
N_EP = 32


def draw_query_rotary(key, part):
    key = jax.random.fold_in(key, 11)
    return jnp.clip(jax.random.normal(key, (STEPS, ROWS, HEADS * ROPE), jnp.float32), -6.0, 6.0).astype(jnp.bfloat16)


def draw_cache_rotary(key, part):
    key = jax.random.fold_in(key, 23)
    return jnp.clip(jax.random.normal(key, (ROWS, ROPE, LMAX), jnp.float32), -6.0, 6.0).astype(jnp.bfloat16)


def draw_lengths(key, part):
    key = jax.random.fold_in(key, 5)
    first_key, second_key = jax.random.split(key)
    base = jax.random.randint(first_key, (ROWS,), 2, LMAX + 1, dtype=jnp.int32)
    longest = jax.random.randint(second_key, (), 0, ROWS, dtype=jnp.int32)
    return jnp.where(jnp.arange(ROWS, dtype=jnp.int32) == longest, LMAX, base).astype(jnp.int32)


def level_of(own_key, dims, cuts, smallest, top_value):
    def one(position, parts):
        draws = jax.random.uniform(jax.random.fold_in(jax.random.fold_in(own_key, 6), position), (parts,), jnp.float32, smallest / len(cuts), top_value / len(cuts))
        return jnp.repeat(jnp.exp(draws), dims[position] // parts).reshape((-1,) + (1,) * (len(dims) - position - 1))

    loudness = one(*cuts[0])
    for cut in cuts[1:]:
        loudness = loudness * one(*cut)
    return loudness


def deal_out(stream_key, own, number, rows, amount, top, bound, lean):
    order = jax.random.permutation(stream_key, amount)
    packed, ordinary = load_shares(amount, rows * top, bound, lean, True), load_shares(amount, rows * top, bound, lean, False)
    places = jnp.arange(amount)

    def named(tallies, offset_by):
        used = int((tallies > 0).sum())
        fixed = max(1, used // 4)
        passed = fixed + (places - fixed + offset_by * (used - fixed)) % max(1, amount - fixed)
        return jnp.zeros((amount,), jnp.int32).at[order[jnp.where(places < fixed, places, passed)]].set(jnp.asarray(tallies, jnp.int32))

    tallies = jnp.where(number % 4 == 0, named(packed, number // 4), named(ordinary, number - number // 4 - 1))
    mixed = jax.random.permutation(jax.random.fold_in(own, 3), amount)
    giver, taker = mixed[0:amount // 2 * 2:2], mixed[1:amount // 2 * 2:2]
    margin = jnp.minimum(tallies[giver] - 1, bound - tallies[taker]) // 2
    margin = jnp.where((giver == order[0]) | (taker == order[0]) | (tallies[taker] == 0), 0, jnp.maximum(margin, 0))
    passed = jax.random.randint(jax.random.fold_in(own, 4), (amount // 2,), 0, 1 << 20) % (margin + 1)
    tallies = tallies.at[giver].add(-passed).at[taker].add(passed)
    labels = jnp.searchsorted(jnp.cumsum(tallies), jnp.arange(rows * top), side="right").astype(jnp.int32)
    table = labels.reshape(top, rows).T
    table = table[jax.random.permutation(jax.random.fold_in(own, 1), rows)]
    offset_by = jax.random.randint(jax.random.fold_in(own, 2), (rows, 1), 0, top)
    return jnp.take_along_axis(table, (jnp.arange(top)[None, :] + offset_by) % top, axis=1)


def load_shares(number_of, total, bound, lean, full):
    loads = [(1 << 20) // math.isqrt(rank ** lean) + 1 for rank in range(1, number_of + 1)]
    largest = bound if full else min(bound, max(-(-total // number_of), total * loads[0] // sum(loads)))
    least = 1 if total - largest >= number_of - 1 else 0
    given, spare = [largest] + [least] * (number_of - 1), total - largest - least * (number_of - 1)
    while spare > 0:
        movable = [i for i in range(1, number_of) if given[i] < largest] or [i for i in range(1, number_of) if given[i] < bound]
        pool, left = sum([loads[i] for i in movable]), spare
        for i in movable:
            addition = min(bound - given[i], max(1, left * loads[i] // pool), spare)
            given[i] = given[i] + addition
            spare = spare - addition
    return np.array(given)


def normal_values(stream_key, dims, spread, reach, cuts=(), kind=jnp.bfloat16):
    values = jax.random.normal(stream_key, dims, jnp.float32) * spread
    if len(cuts) > 0:
        values = level_of(stream_key, dims, cuts, -0.22, 0.18) * values
    return jnp.clip(values, min=-reach, max=reach).astype(kind)


def setup_inputs(seed: int = 0) -> dict:
    splits = jax.random.split(jax.random.key(seed), 18)
    query_plain = normal_values(splits[0], (STEPS, ROWS, HEADS * NOPE), 1.0, 6.0, ((1, 4), (2, 32)))
    query_rotary = draw_query_rotary(jax.random.fold_in(splits[17], 71), 0)
    key_up = normal_values(splits[2], (HEADS, NOPE, LAT), NOPE ** -0.5, 0.5, ((0, 32),))
    value_up = normal_values(splits[3], (HEADS, LAT, VHEAD), LAT ** -0.5, 0.25, ((0, 32),))
    output_weight = normal_values(splits[4], (HEADS * VHEAD, D), (HEADS * VHEAD) ** -0.5, 0.0625, ((0, 32),))
    cache_latent = normal_values(splits[5], (ROWS, LMAX, LAT), 1.0, 6.0, ((0, 128),))
    cache_rotary = draw_cache_rotary(jax.random.fold_in(splits[17], 71), 0)
    lengths = draw_lengths(jax.random.fold_in(splits[17], 71), 0)
    new_latent = normal_values(splits[8], (STEPS, ROWS, LAT), 1.0, 6.0, ((1, 128),))
    new_rotary = normal_values(splits[9], (STEPS, ROWS, ROPE), 1.0, 6.0, ((1, 128),))
    residual = normal_values(splits[10], (STEPS, ROWS, D), 0.25, 1.5, ((1, 128),))
    norm_gain = jnp.clip(1.0 + 0.1 * jax.random.normal(splits[11], (D,), jnp.float32), 0.5, 1.5)
    expert_ids_keys = jax.random.split(jax.random.fold_in(splits[12], 1), STEPS * ROWS // ROWS_DEV)
    expert_ids_turns = jax.random.permutation(jax.random.fold_in(splits[12], 3), STEPS * ROWS // ROWS_DEV)
    expert_ids = jax.vmap(lambda own, number: deal_out(jax.random.fold_in(splits[12], 2), own, number, ROWS_DEV, EXPERTS, TOP, MOST, 2))(expert_ids_keys, expert_ids_turns).reshape((STEPS, ROWS, TOP))
    gate_weights = jnp.clip(0.05 + 0.45 * jax.random.uniform(splits[13], (STEPS, ROWS, TOP), jnp.float32) ** level_of(splits[13], (STEPS, ROWS, TOP), ((1, 128),), -0.2, 0.2), 0.05, 0.5)
    expert_gate = normal_values(splits[14], (EXPERTS, D, HID), D ** -0.5, 0.09375, ((0, 128),))
    expert_up = normal_values(splits[15], (EXPERTS, D, HID), D ** -0.5, 0.09375, ((0, 128),))
    expert_down = normal_values(splits[16], (EXPERTS, HID, D), HID ** -0.5, 0.1875, ((0, 128),))
    return {"query_plain": query_plain, "query_rotary": query_rotary, "key_up": key_up, "value_up": value_up, "output_weight": output_weight, "cache_latent": cache_latent, "cache_rotary": cache_rotary, "lengths": lengths, "new_latent": new_latent, "new_rotary": new_rotary, "residual": residual, "norm_gain": norm_gain, "expert_ids": expert_ids, "gate_weights": gate_weights, "expert_gate": expert_gate, "expert_up": expert_up, "expert_down": expert_down}


def expert_layer(normed, chosen, weights, expert_gate, expert_up, expert_down):
    flat_ids = chosen.reshape(-1).astype(jnp.int32)
    flat_weights = weights.reshape(-1)
    order = jnp.argsort(flat_ids, stable=True).astype(jnp.int32)
    catalog = jnp.arange(EXPERTS, dtype=jnp.int32)
    counts = lax.optimization_barrier(jnp.sum((flat_ids[:, None] == catalog[None, :]).astype(jnp.int32), axis=0)).astype(jnp.int32)
    offsets = (jnp.cumsum(counts) - counts).astype(jnp.int32)
    padded = jnp.concatenate([order, jnp.zeros((32,), jnp.int32)])
    lanes = jnp.arange(32, dtype=jnp.int32)

    def one_expert(expert, total):
        count = counts[expert]
        start = offsets[expert]

        def one_piece(piece, inner):
            picks = lax.dynamic_slice(padded, (start + piece * 32,), (32,))
            live = lanes + piece * 32 < count
            source = (picks // TOP).astype(jnp.int32)
            inputs = normed[source]
            gate = jnp.dot(inputs, expert_gate[expert], preferred_element_type=jnp.float32)
            upward = jnp.dot(inputs, expert_up[expert], preferred_element_type=jnp.float32)
            hidden = (jax.nn.silu(gate) * upward).astype(jnp.bfloat16)
            result = jnp.dot(hidden, expert_down[expert], preferred_element_type=jnp.float32).astype(jnp.bfloat16)
            scaled = jnp.where(live, flat_weights[picks], jnp.zeros_like(flat_weights[picks]))
            return inner.at[source].add(scaled[:, None] * result.astype(jnp.float32))
        return lax.fori_loop(jnp.int32(0), ((count + 31) // 32).astype(jnp.int32), one_piece, total)
    return lax.fori_loop(jnp.int32(0), jnp.int32(EXPERTS), one_expert, jnp.zeros(normed.shape, jnp.float32))

def reference(query_plain, query_rotary, key_up, value_up, output_weight, cache_latent, cache_rotary, lengths, new_latent, new_rotary, residual, norm_gain, expert_ids, gate_weights, expert_gate, expert_up, expert_down):
    scale = 1.0 / (NOPE + ROPE) ** 0.5
    head_local = HEADS // N_EP
    latents = cache_latent.astype(jnp.float32)
    rotary_keys = cache_rotary.astype(jnp.float32)
    fresh_latent = jnp.swapaxes(new_latent, 0, 1).astype(jnp.float32)
    fresh_rotary = jnp.swapaxes(new_rotary, 0, 1).astype(jnp.float32)
    visible = jnp.arange(LMAX, dtype=jnp.int32)[None, :] < lengths[:, None]
    sections = jnp.arange(STEPS, dtype=jnp.int32)
    key_map = key_up.astype(jnp.float32)
    value_map = value_up.astype(jnp.float32)
    results = []
    for current in range(STEPS):
        plain = query_plain[current].reshape(ROWS, HEADS, NOPE).astype(jnp.float32)
        absorbed = jnp.einsum('rhn,hnl->rhl', plain, key_map).astype(jnp.bfloat16).astype(jnp.float32)
        rotary = query_rotary[current].reshape(ROWS, HEADS, ROPE).astype(jnp.float32)
        cached = (jnp.einsum('rhl,rpl->rhp', absorbed, latents) + jnp.einsum('rhe,rep->rhp', rotary, rotary_keys)) * scale
        fresh = (jnp.einsum('rhl,rjl->rhj', absorbed, fresh_latent) + jnp.einsum('rhe,rje->rhj', rotary, fresh_rotary)) * scale
        cached = jnp.where(visible[:, None, :], cached, -jnp.inf)
        fresh = jnp.where((sections <= current)[None, None, :], fresh, -jnp.inf)
        peak = jnp.maximum(lax.optimization_barrier(jnp.max(cached, axis=-1)), lax.optimization_barrier(jnp.max(fresh, axis=-1)))[..., None]
        cached_exp = jnp.exp(cached - peak)
        fresh_exp = jnp.exp(fresh - peak)
        total = lax.optimization_barrier(jnp.sum(cached_exp, axis=-1, keepdims=True)) + lax.optimization_barrier(jnp.sum(fresh_exp, axis=-1, keepdims=True))
        cached_prob = (cached_exp / total).astype(jnp.bfloat16).astype(jnp.float32)
        fresh_prob = (fresh_exp / total).astype(jnp.bfloat16).astype(jnp.float32)
        mixed = jnp.einsum('rhp,rpl->rhl', cached_prob, latents) + jnp.einsum('rhj,rjl->rhl', fresh_prob, fresh_latent)
        mixed = mixed.astype(jnp.bfloat16).astype(jnp.float32)
        values = jnp.einsum('rhl,hlv->rhv', mixed, value_map).astype(jnp.bfloat16)
        attention = jnp.zeros((ROWS, D), jnp.float32)
        for group in range(N_EP):
            span = values[:, group * head_local:(group + 1) * head_local, :].reshape(ROWS, head_local * VHEAD)
            rows_of = output_weight[group * head_local * VHEAD:(group + 1) * head_local * VHEAD]
            part = jnp.dot(span, rows_of, preferred_element_type=jnp.float32).astype(jnp.bfloat16)
            attention = attention + part.astype(jnp.float32)
        hidden = residual[current].astype(jnp.float32) + attention
        normed = (hidden * lax.rsqrt(lax.optimization_barrier(jnp.mean(hidden * hidden, axis=-1, keepdims=True)) + 1e-06) * norm_gain).astype(jnp.bfloat16)
        routed = expert_layer(normed, expert_ids[current], gate_weights[current], expert_gate, expert_up, expert_down)
        results.append((hidden + routed).astype(jnp.bfloat16))
    return jnp.stack(results)
```

```python
import jax
import jax.numpy as jnp
from jax import lax
from jax.sharding import PartitionSpec as P

D = 3584
HEADS = 64
LAT = 512
ROPE = 64
NOPE = 128
VHEAD = 128
MOST = 2
STEPS = 4
EXPERTS = 128
LMAX = 64
ROWS_DEV = 4
CHIPS = 16
HC = 4
RS = STEPS * ROWS_DEV

SAME_CORE = [[2 * chip + core for chip in range(CHIPS)] for core in range(2)]
OTHER_CORE = [(i, i ^ 1) for i in range(2 * CHIPS)]


def other_core(x):
    return lax.ppermute(x, "ep", OTHER_CORE)


def exchange(x):
    return lax.all_to_all(x, "ep", 0, 0, tiled=True, axis_index_groups=SAME_CORE)


def attend(absorbed, rotary, cache_latent, cache_rotary, lengths, new_latent, new_rotary):
    scale = 1.0 / (NOPE + ROPE) ** 0.5
    f32 = jnp.float32
    cached = jnp.einsum("clqd,lpd->lcqp", absorbed, cache_latent, preferred_element_type=f32)
    cached = cached + jnp.einsum("clqe,lep->lcqp", rotary, cache_rotary, preferred_element_type=f32)
    fresh = jnp.einsum("clqd,jld->lcqj", absorbed, new_latent, preferred_element_type=f32)
    fresh = fresh + jnp.einsum("clqe,jle->lcqj", rotary, new_rotary, preferred_element_type=f32)
    visible = jnp.arange(LMAX, dtype=jnp.int32)[None, :] < lengths[:, None]
    step = jnp.arange(HC * STEPS, dtype=jnp.int32) % STEPS
    known = jnp.arange(STEPS, dtype=jnp.int32)[None, :] <= step[:, None]
    cached = jnp.where(visible[:, None, None, :], cached * scale, -jnp.inf)
    fresh = jnp.where(known[None, None], fresh * scale, -jnp.inf)
    peak = jnp.maximum(jnp.max(cached, axis=-1), jnp.max(fresh, axis=-1))[..., None]
    cached = jnp.exp(cached - peak)
    fresh = jnp.exp(fresh - peak)
    total = jnp.sum(cached, axis=-1, keepdims=True) + jnp.sum(fresh, axis=-1, keepdims=True)
    cached = (cached / total).astype(jnp.bfloat16)
    fresh = (fresh / total).astype(jnp.bfloat16)
    mixed = jnp.einsum("lcqp,lpd->clqd", cached, cache_latent, preferred_element_type=f32)
    mixed = mixed + jnp.einsum("lcqj,jld->clqd", fresh, new_latent, preferred_element_type=f32)
    return mixed.astype(jnp.bfloat16)


def per_device(
    query_plain,
    query_rotary,
    key_up,
    value_up,
    output_weight,
    cache_latent,
    cache_rotary,
    lengths,
    new_latent,
    new_rotary,
    residual,
    norm_gain,
    expert_ids,
    gate_weights,
    expert_gate,
    expert_up,
    expert_down,
):
    f32 = jnp.float32
    bf16 = jnp.bfloat16
    core = lax.axis_index("ep") % 2
    expert = lax.axis_index("dp") * lax.axis_size("ep") + lax.axis_index("ep")

    ids = jnp.swapaxes(expert_ids, 0, 1).reshape(RS, -1)
    weights = jnp.swapaxes(gate_weights, 0, 1).reshape(RS, -1)
    meta = jnp.concatenate([ids.astype(f32), weights], axis=1)
    meta = lax.all_gather(meta, ("dp", "ep"), axis=0, tiled=True)

    queries = jnp.concatenate([query_plain, query_rotary], axis=2)
    queries = queries.reshape(STEPS, CHIPS, 2, ROWS_DEV, 2 * (NOPE + ROPE))
    kept = lax.dynamic_index_in_dim(queries, core, axis=2, keepdims=False)
    given = lax.dynamic_index_in_dim(queries, 1 - core, axis=2, keepdims=False)
    given = other_core(given)
    key_map = jnp.concatenate([key_up, other_core(key_up)], axis=0)
    value_map = jnp.concatenate([value_up, other_core(value_up)], axis=0)
    out_map = jnp.concatenate([output_weight, other_core(output_weight)], axis=0)
    split = 2 * NOPE
    plain = jnp.stack([kept[..., :split], given[..., :split]], axis=3)
    plain = plain.reshape(STEPS, CHIPS, ROWS_DEV, HC, NOPE)
    rotary = jnp.stack([kept[..., split:], given[..., split:]], axis=3)
    rotary = rotary.reshape(STEPS, CHIPS, ROWS_DEV, HC, ROPE)
    absorbed = jnp.einsum("sclhn,hnd->clhsd", plain, key_map, preferred_element_type=f32)
    absorbed = absorbed.astype(bf16).reshape(CHIPS, ROWS_DEV, HC * STEPS, LAT)
    rotary = jnp.transpose(rotary, (1, 2, 3, 0, 4)).reshape(CHIPS, ROWS_DEV, HC * STEPS, ROPE)
    sent = exchange(jnp.concatenate([absorbed, rotary], axis=3))
    mixed = attend(
        sent[..., :LAT],
        sent[..., LAT:],
        cache_latent,
        cache_rotary,
        lengths,
        new_latent,
        new_rotary,
    )
    mixed = exchange(mixed).reshape(CHIPS, ROWS_DEV, HC, STEPS, LAT)
    values = jnp.einsum("clhsd,hdv->clshv", mixed, value_map, preferred_element_type=f32)
    values = values.astype(bf16).reshape(CHIPS * RS, HC * VHEAD)
    parts = jnp.dot(values, out_map, preferred_element_type=f32).astype(bf16)
    parts = exchange(parts.reshape(CHIPS, RS, D))
    attention = jnp.sum(parts.astype(f32), axis=0)
    hidden = jnp.swapaxes(residual, 0, 1).reshape(RS, D).astype(f32) + attention
    normed = (
        hidden * lax.rsqrt(jnp.mean(hidden * hidden, axis=-1, keepdims=True) + 1e-06) * norm_gain
    ).astype(bf16)

    rows = lax.all_gather(normed, ("dp", "ep"), axis=0, tiled=True)
    same = meta[:, :8] == expert.astype(f32)
    weight = jnp.sum(jnp.where(same, meta[:, 8:], 0.0), axis=1)
    named = jnp.any(same, axis=1).astype(jnp.int32).reshape(EXPERTS, ROWS_DEV, STEPS)
    rank = jnp.cumsum(named, axis=1) - named
    place = jnp.arange(EXPERTS, dtype=jnp.int32)[:, None, None] % 16 * (MOST * STEPS)
    place = place + jnp.arange(STEPS, dtype=jnp.int32)[None, None, :] * MOST + rank
    place = jnp.where(named > 0, place, -1).reshape(8, 1, 256)
    pick = place == jnp.arange(128, dtype=jnp.int32)[None, :, None]
    slot_weight = jnp.sum(jnp.where(pick, weight.reshape(8, 1, 256), 0.0), axis=2)
    slots = jnp.einsum(
        "tsr,trd->tsd", pick.astype(bf16), rows.reshape(8, 256, D), preferred_element_type=f32
    )
    slots = slots.astype(bf16).reshape(8 * 128, D)
    gate = jnp.dot(slots, expert_gate[0], preferred_element_type=f32)
    upward = jnp.dot(slots, expert_up[0], preferred_element_type=f32)
    inner = (jax.nn.silu(gate) * upward).astype(bf16)
    result = jnp.dot(inner, expert_down[0], preferred_element_type=f32)
    result = (result * slot_weight.reshape(-1, 1)).astype(bf16)

    back = lax.all_to_all(
        result.reshape(EXPERTS, MOST * STEPS, D), ("dp", "ep"), 0, 0, tiled=True
    ).reshape(EXPERTS * MOST * STEPS, D)
    chosen = ids.reshape(ROWS_DEV, STEPS, -1)
    earlier = jnp.tril(jnp.ones((ROWS_DEV, ROWS_DEV), jnp.int32), -1)
    twins = jnp.any(chosen[:, None, :, :, None] == chosen[None, :, :, None, :], axis=-1)
    rank = jnp.sum(twins.astype(jnp.int32) * earlier[:, :, None, None], axis=1)
    target = chosen * (MOST * STEPS) + rank
    target = target + jnp.arange(STEPS, dtype=jnp.int32)[None, :, None] * MOST
    target = target.reshape(RS, -1, 1)
    slot_index = jnp.arange(EXPERTS * MOST * STEPS, dtype=jnp.int32)
    take = jnp.any(target == slot_index[None, None, :], axis=1).astype(bf16)
    routed = jnp.dot(take, back, preferred_element_type=f32)
    out = (hidden + routed).astype(bf16)
    return jnp.swapaxes(out.reshape(ROWS_DEV, STEPS, D), 0, 1)


def solution(mesh):
    return jax.shard_map(
        per_device,
        mesh=mesh,
        in_specs=(
            P(None, "dp", "ep"),
            P(None, "dp", "ep"),
            P("ep", None, None),
            P("ep", None, None),
            P("ep", None),
            P(("dp", "ep"), None, None),
            P(("dp", "ep"), None, None),
            P(("dp", "ep")),
            P(None, ("dp", "ep"), None),
            P(None, ("dp", "ep"), None),
            P(None, ("dp", "ep"), None),
            P(),
            P(None, ("dp", "ep"), None),
            P(None, ("dp", "ep"), None),
            P(("dp", "ep"), None, None),
            P(("dp", "ep"), None, None),
            P(("dp", "ep"), None, None),
        ),
        out_specs=P(None, ("dp", "ep"), None),
        check_vma=False,
    )
```

```python
import functools

import jax
import jax.numpy as jnp
import numpy as np
from jax import lax
from jax.experimental import pallas as pl
from jax.experimental.pallas import tpu as pltpu
from jax.sharding import PartitionSpec as P

D = 3584
HEADS = 64
LAT = 512
ROPE = 64
NOPE = 128
VHEAD = 128
MOST = 2
TOP = 8
BLOCK = 256
SLOTS = 128
BESIDE = 128
STEPS = 4
EXPERTS = 128
LMAX = 64
ROWS_DEV = 4
CHIPS = 16
HC = 4
RS = STEPS * ROWS_DEV

SAME_CORE = [[2 * chip + core for chip in range(CHIPS)] for core in range(2)]
OTHER_CORE = [(i, i ^ 1) for i in range(2 * CHIPS)]
PLANES = [
    [y * 32 + first * unit + second * (10 - unit) + core for second in range(4) for y in range(4)]
    for core, unit in ((0, 8), (1, 2))
    for first in range(4)
]


SEATS = MOST * STEPS


def place_of(axis):
    group = lax.axis_index("ep")
    return {"y": lax.axis_index("dp"), "x": group // 8, "z": group // 2 % 4}[axis]


def shift(x, turn, by):
    if turn == 2:
        return lax.ppermute(x, "dp", [(i, (i + by) % 4) for i in range(4)])
    pairs = []
    for i in range(2 * CHIPS):
        unit = 8 if i % 2 == turn else 2
        pairs.append((i, i + ((i // unit + by) % 4 - i // unit % 4) * unit))
    return lax.ppermute(x, "ep", pairs)


def plane_exchange(x):
    return lax.all_to_all(x, ("dp", "ep"), 0, 0, tiled=True, axis_index_groups=PLANES)


def routing(expert_ids, gate_weights):
    ids = jnp.swapaxes(expert_ids, 0, 1).reshape(RS, -1).astype(jnp.float32)
    rest = jnp.swapaxes(gate_weights, 0, 1).reshape(RS, -1)
    columns = [ids]
    for _ in range(3):
        columns.append(lax.reduce_precision(rest, 8, 7))
        rest = rest - columns[-1]
    columns = jnp.concatenate(columns, axis=1)
    return jnp.pad(columns, ((0, 0), (0, BESIDE - columns.shape[1]))).astype(jnp.bfloat16)


def pick_kernel(pieces, experts, *refs):
    f32 = jnp.float32
    count = sum(pieces) // BLOCK
    columns, rows = refs[: len(pieces)], refs[len(pieces) : 2 * len(pieces)]
    picked, put, weight = refs[-4:-2], refs[-2], refs[-1]

    @pl.when(pl.program_id(0) == 0)
    def _():
        shape = (BLOCK, BLOCK)
        this, other = (lax.broadcasted_iota(jnp.int32, shape, i) for i in (0, 1))
        earlier = (
            (this // RS == other // RS)
            & (this % STEPS == other % STEPS)
            & (this % RS // STEPS > other % RS // STEPS)
        ).astype(jnp.bfloat16)
        shape = (BLOCK, BESIDE)
        row, lane = (lax.broadcasted_iota(jnp.int32, shape, i) for i in (0, 1))
        base = (row // RS * SEATS + row % STEPS * MOST).astype(f32)
        beside = jnp.concatenate([c[...] for c in columns], axis=0).astype(f32)
        for block in range(count):
            ids = beside[block * BLOCK : (block + 1) * BLOCK]
            weights = sum(pltpu.roll(ids, BESIDE - i * TOP, 1) for i in (1, 2, 3))
            for i in range(2):
                same = (ids == experts[i].astype(f32)) & (lane < TOP)
                amount = jnp.sum(jnp.where(same, weights, 0.0), axis=1, keepdims=True)
                named = jnp.max(jnp.where(same, 1.0, 0.0), axis=1, keepdims=True)
                named = jnp.broadcast_to(named, shape)
                rank = jnp.dot(earlier, named.astype(jnp.bfloat16), preferred_element_type=f32)
                seat = jnp.where(named > 0.0, rank + base, -1.0)
                put[block, i] = jnp.where(seat == lane.astype(f32), 1.0, 0.0).astype(jnp.bfloat16)
                weight[block, i] = jnp.broadcast_to(amount, shape)

    x = jnp.concatenate([r[...] for r in rows], axis=0)
    for block in range(count):
        for i in range(2):
            slots = lax.dot_general(
                put[block, i],
                x[block * BLOCK : (block + 1) * BLOCK],
                (((0,), (0,)), ((), ())),
                preferred_element_type=f32,
            )
            picked[i][block * SLOTS : (block + 1) * SLOTS] = slots.astype(jnp.bfloat16)


def pick(experts, pieces, after=()):
    sizes = tuple(p.shape[0] for p in pieces)
    blocks = sum(sizes) // BLOCK
    tile = 512
    spec = pl.BlockSpec((blocks, 2, BLOCK, SLOTS), lambda i: (0, 0, 0, 0))
    out = pl.BlockSpec((blocks * SLOTS, tile), lambda i: (0, i))
    return pl.pallas_call(
        functools.partial(pick_kernel, sizes),
        grid=(D // tile,),
        in_specs=[pl.BlockSpec(memory_space=pltpu.SMEM)]
        + [pl.BlockSpec((n, BESIDE), lambda i: (0, D // BESIDE)) for n in sizes]
        + [pl.BlockSpec((n, tile), lambda i: (0, i)) for n in sizes]
        + [pl.BlockSpec(memory_space=pl.ANY) for _ in after],
        out_specs=[out, out, spec, spec],
        out_shape=[
            jax.ShapeDtypeStruct((blocks * SLOTS, D), jnp.bfloat16),
            jax.ShapeDtypeStruct((blocks * SLOTS, D), jnp.bfloat16),
            jax.ShapeDtypeStruct((blocks, 2, BLOCK, SLOTS), jnp.bfloat16),
            jax.ShapeDtypeStruct((blocks, 2, BLOCK, SLOTS), jnp.float32),
        ],
        compiler_params=pltpu.CompilerParams(vmem_limit_bytes=40 * 2**20),
    )(experts, *pieces, *pieces, *after)


def experts_kernel(own, twin, gate, upward, down, out, total):
    f32 = jnp.float32
    tile = pl.program_id(0)
    half = own.shape[0]

    @pl.when(tile == 0)
    def _():
        total[...] = jnp.zeros_like(total)

    x = jnp.concatenate([own[...], twin[...]], axis=0)
    g = jnp.dot(x, gate[0], preferred_element_type=f32)
    u = jnp.dot(x, upward[0], preferred_element_type=f32)
    inner = (g / (1.0 + jnp.exp(-g)) * u).astype(jnp.bfloat16)
    total[...] += jnp.dot(inner, down[0], preferred_element_type=f32)

    @pl.when(tile == pl.num_programs(0) - 1)
    def _():
        out[0] = total[:half].astype(jnp.bfloat16)
        out[1] = total[half:].astype(jnp.bfloat16)


def run_experts(own, twin, gate, upward, down, tile=256):
    rows, hidden = own.shape[0], gate.shape[2]
    whole = pl.BlockSpec((rows, D), lambda i: (0, 0))
    return pl.pallas_call(
        experts_kernel,
        grid=(hidden // tile,),
        in_specs=[
            whole,
            whole,
            pl.BlockSpec((1, D, tile), lambda i: (0, 0, i)),
            pl.BlockSpec((1, D, tile), lambda i: (0, 0, i)),
            pl.BlockSpec((1, tile, D), lambda i: (0, i, 0)),
        ],
        out_specs=pl.BlockSpec((2, rows, D), lambda i: (0, 0, 0)),
        out_shape=jax.ShapeDtypeStruct((2, rows, D), jnp.bfloat16),
        scratch_shapes=[pltpu.VMEM((2 * rows, D), jnp.float32)],
        compiler_params=pltpu.CompilerParams(vmem_limit_bytes=40 * 2**20),
        cost_estimate=pl.CostEstimate(flops=rows * D, bytes_accessed=rows * D, transcendentals=0),
    )(own, twin, gate, upward, down)


def other_core(x):
    return lax.ppermute(x, "ep", OTHER_CORE)


def exchange(x):
    return lax.all_to_all(x, "ep", 0, 0, tiled=True, axis_index_groups=SAME_CORE)


def attend(absorbed, rotary, cache_latent, cache_rotary, lengths, new_latent, new_rotary):
    scale = 1.0 / (NOPE + ROPE) ** 0.5
    f32 = jnp.float32
    cached = jnp.einsum("clqd,lpd->lcqp", absorbed, cache_latent, preferred_element_type=f32)
    cached = cached + jnp.einsum("clqe,lep->lcqp", rotary, cache_rotary, preferred_element_type=f32)
    fresh = jnp.einsum("clqd,jld->lcqj", absorbed, new_latent, preferred_element_type=f32)
    fresh = fresh + jnp.einsum("clqe,jle->lcqj", rotary, new_rotary, preferred_element_type=f32)
    visible = jnp.arange(LMAX, dtype=jnp.int32)[None, :] < lengths[:, None]
    step = jnp.arange(HC * STEPS, dtype=jnp.int32) % STEPS
    known = jnp.arange(STEPS, dtype=jnp.int32)[None, :] <= step[:, None]
    cached = jnp.where(visible[:, None, None, :], cached * scale, -jnp.inf)
    fresh = jnp.where(known[None, None], fresh * scale, -jnp.inf)
    peak = jnp.maximum(jnp.max(cached, axis=-1), jnp.max(fresh, axis=-1))[..., None]
    cached = jnp.exp(cached - peak)
    fresh = jnp.exp(fresh - peak)
    total = jnp.sum(cached, axis=-1, keepdims=True) + jnp.sum(fresh, axis=-1, keepdims=True)
    cached = (cached / total).astype(jnp.bfloat16)
    fresh = (fresh / total).astype(jnp.bfloat16)
    mixed = jnp.einsum("lcqp,lpd->clqd", cached, cache_latent, preferred_element_type=f32)
    mixed = mixed + jnp.einsum("lcqj,jld->clqd", fresh, new_latent, preferred_element_type=f32)
    return mixed.astype(jnp.bfloat16)


def per_device(
    query_plain,
    query_rotary,
    key_up,
    value_up,
    output_weight,
    cache_latent,
    cache_rotary,
    lengths,
    new_latent,
    new_rotary,
    residual,
    norm_gain,
    expert_ids,
    gate_weights,
    expert_gate,
    expert_up,
    expert_down,
):
    f32 = jnp.float32
    bf16 = jnp.bfloat16
    core = lax.axis_index("ep") % 2
    expert = lax.axis_index("dp") * lax.axis_size("ep") + lax.axis_index("ep")

    queries = jnp.concatenate([query_plain, query_rotary], axis=2)
    queries = queries.reshape(STEPS, CHIPS, 2, ROWS_DEV, 2 * (NOPE + ROPE))
    kept = lax.dynamic_index_in_dim(queries, core, axis=2, keepdims=False)
    given = lax.dynamic_index_in_dim(queries, 1 - core, axis=2, keepdims=False)
    given = other_core(given)
    key_map = jnp.concatenate([key_up, other_core(key_up)], axis=0)
    value_map = jnp.concatenate([value_up, other_core(value_up)], axis=0)
    out_map = jnp.concatenate([output_weight, other_core(output_weight)], axis=0)
    split = 2 * NOPE
    plain = jnp.stack([kept[..., :split], given[..., :split]], axis=3)
    plain = plain.reshape(STEPS, CHIPS, ROWS_DEV, HC, NOPE)
    rotary = jnp.stack([kept[..., split:], given[..., split:]], axis=3)
    rotary = rotary.reshape(STEPS, CHIPS, ROWS_DEV, HC, ROPE)
    absorbed = jnp.einsum("sclhn,hnd->clhsd", plain, key_map, preferred_element_type=f32)
    absorbed = absorbed.astype(bf16).reshape(CHIPS, ROWS_DEV, HC * STEPS, LAT)
    rotary = jnp.transpose(rotary, (1, 2, 3, 0, 4)).reshape(CHIPS, ROWS_DEV, HC * STEPS, ROPE)
    sent = exchange(jnp.concatenate([absorbed, rotary], axis=3))
    mixed = attend(
        sent[..., :LAT],
        sent[..., LAT:],
        cache_latent,
        cache_rotary,
        lengths,
        new_latent,
        new_rotary,
    )
    mixed = exchange(mixed).reshape(CHIPS, ROWS_DEV, HC, STEPS, LAT)
    values = jnp.einsum("clhsd,hdv->clshv", mixed, value_map, preferred_element_type=f32)
    values = values.astype(bf16).reshape(CHIPS * RS, HC * VHEAD)
    parts = jnp.dot(values, out_map, preferred_element_type=f32).astype(bf16)
    parts = exchange(parts.reshape(CHIPS, RS, D))
    attention = jnp.sum(parts.astype(f32), axis=0)
    hidden = jnp.swapaxes(residual, 0, 1).reshape(RS, D).astype(f32) + attention
    normed = (
        hidden * lax.rsqrt(jnp.mean(hidden * hidden, axis=-1, keepdims=True) + 1e-06) * norm_gain
    ).astype(bf16)

    pair = jnp.stack([expert, expert ^ 1])

    def experts(own, twin):
        return run_experts(own, other_core(twin), expert_gate, expert_up, expert_down)

    def spread(put, weight, own, twin):
        total = 0.0
        for i, half in enumerate((own, twin)):
            back = jnp.dot(put[i], half, preferred_element_type=f32)
            total = total + back * weight[i, :, :1]
        return total.astype(bf16)

    rows = jnp.concatenate([normed, routing(expert_ids, gate_weights)], axis=1)
    rows = plane_exchange(jnp.broadcast_to(rows[None], (16, RS, D + BESIDE)))
    rows = rows.reshape(BLOCK, D + BESIDE)
    half = BLOCK // 2
    before = shift(rows, 0, 1)
    after = shift(rows, 0, -1)
    far = [shift(before[:half], 0, 1), shift(after[half:], 0, -1)]
    own, twin, put, weight = pick(pair, [rows])
    result = experts(own, twin)
    own_sum = spread(put[0], weight[0], result[0], other_core(result[1]))
    own, twin, put, weight = pick(pair, [after, before], [result])
    result = experts(own, twin)
    own, twin = result[0], other_core(result[1])
    after, before = (
        spread(put[i], weight[i], own[i * SLOTS :][:SLOTS], twin[i * SLOTS :][:SLOTS])
        for i in range(2)
    )
    own, twin, put, weight = pick(pair, far, [result])
    result = experts(own, twin)
    far = spread(put[0], weight[0], result[0], other_core(result[1]))

    up = shift(far[:half], 0, 1)
    down = shift(far[half:], 0, -1)
    after = jnp.concatenate([after[:half] + up, after[half:]], axis=0)
    before = jnp.concatenate([before[:half], before[half:] + down], axis=0)
    after = shift(after, 0, 1)
    before = shift(before, 0, -1)
    total = own_sum.astype(f32) + after.astype(f32) + before.astype(f32)
    routed = plane_exchange(total.astype(bf16).reshape(16, RS, D))
    out = (hidden + jnp.sum(routed.astype(f32), axis=0)).astype(bf16)
    return jnp.swapaxes(out.reshape(ROWS_DEV, STEPS, D), 0, 1)


def solution(mesh):
    return jax.shard_map(
        per_device,
        mesh=mesh,
        in_specs=(
            P(None, "dp", "ep"),
            P(None, "dp", "ep"),
            P("ep", None, None),
            P("ep", None, None),
            P("ep", None),
            P(("dp", "ep"), None, None),
            P(("dp", "ep"), None, None),
            P(("dp", "ep")),
            P(None, ("dp", "ep"), None),
            P(None, ("dp", "ep"), None),
            P(None, ("dp", "ep"), None),
            P(),
            P(None, ("dp", "ep"), None),
            P(None, ("dp", "ep"), None),
            P(("dp", "ep"), None, None),
            P(("dp", "ep"), None, None),
            P(("dp", "ep"), None, None),
        ),
        out_specs=P(None, ("dp", "ep"), None),
        check_vma=False,
    )
```

```python
import functools

import jax
import jax.numpy as jnp
import numpy as np
from jax import lax
from jax.experimental import pallas as pl
from jax.experimental.pallas import tpu as pltpu
from jax.sharding import PartitionSpec as P

D = 3584
HEADS = 64
LAT = 512
ROPE = 64
NOPE = 128
VHEAD = 128
MOST = 2
TOP = 8
BLOCK = 256
SLOTS = 128
BESIDE = 128
STEPS = 4
EXPERTS = 128
LMAX = 64
KEYS = 128
ROWS_DEV = 4
CHIPS = 16
HC = 4
RS = STEPS * ROWS_DEV

SAME_CORE = [[2 * chip + core for chip in range(CHIPS)] for core in range(2)]
OTHER_CORE = [(i, i ^ 1) for i in range(2 * CHIPS)]
PLANES = [
    [y * 32 + first * unit + second * (10 - unit) + core for second in range(4) for y in range(4)]
    for core, unit in ((0, 8), (1, 2))
    for first in range(4)
]


SEATS = MOST * STEPS


def place_of(axis):
    group = lax.axis_index("ep")
    return {"y": lax.axis_index("dp"), "x": group // 8, "z": group // 2 % 4}[axis]


def shift(x, turn, by):
    if turn == 2:
        return lax.ppermute(x, "dp", [(i, (i + by) % 4) for i in range(4)])
    pairs = []
    for i in range(2 * CHIPS):
        unit = 8 if i % 2 == turn else 2
        pairs.append((i, i + ((i // unit + by) % 4 - i // unit % 4) * unit))
    return lax.ppermute(x, "ep", pairs)


def plane_exchange(x):
    return lax.all_to_all(x, ("dp", "ep"), 0, 0, tiled=True, axis_index_groups=PLANES)


def routing(expert_ids, gate_weights):
    ids = jnp.swapaxes(expert_ids, 0, 1).reshape(RS, -1).astype(jnp.float32)
    rest = jnp.swapaxes(gate_weights, 0, 1).reshape(RS, -1)
    columns = [ids]
    for _ in range(3):
        columns.append(lax.reduce_precision(rest, 8, 7))
        rest = rest - columns[-1]
    columns = jnp.concatenate(columns, axis=1)
    return jnp.pad(columns, ((0, 0), (0, BESIDE - columns.shape[1]))).astype(jnp.bfloat16)


def pick_kernel(pieces, experts, *refs):
    f32 = jnp.float32
    count = sum(pieces) // BLOCK
    columns, rows = refs[: len(pieces)], refs[len(pieces) : 2 * len(pieces)]
    *picked, put, weight, turned = refs[-5:]

    @pl.when(pl.program_id(0) == 0)
    def _():
        shape = (BLOCK, BLOCK)
        this, other = (lax.broadcasted_iota(jnp.int32, shape, i) for i in (0, 1))
        earlier = (
            (this // RS == other // RS)
            & (this % STEPS == other % STEPS)
            & (this % RS // STEPS > other % RS // STEPS)
        ).astype(jnp.bfloat16)
        shape = (BLOCK, BESIDE)
        row, lane = (lax.broadcasted_iota(jnp.int32, shape, i) for i in (0, 1))
        base = (row // RS * SEATS + row % STEPS * MOST).astype(f32)
        beside = jnp.concatenate([c[...] for c in columns], axis=0).astype(f32)
        for block in range(count):
            ids = beside[block * BLOCK : (block + 1) * BLOCK]
            weights = sum(pltpu.roll(ids, BESIDE - i * TOP, 1) for i in (1, 2, 3))
            for i in range(2):
                same = (ids == experts[i].astype(f32)) & (lane < TOP)
                amount = jnp.sum(jnp.where(same, weights, 0.0), axis=1, keepdims=True)
                named = jnp.max(jnp.where(same, 1.0, 0.0), axis=1, keepdims=True)
                named = jnp.broadcast_to(named, shape)
                rank = jnp.dot(earlier, named.astype(jnp.bfloat16), preferred_element_type=f32)
                seat = jnp.where(named > 0.0, rank + base, -1.0)
                put[block, i] = jnp.where(seat == lane.astype(f32), 1.0, 0.0).astype(jnp.bfloat16)
                seat = jnp.transpose(seat)
                slot = lax.broadcasted_iota(jnp.int32, seat.shape, 0).astype(f32)
                turned[block, i] = jnp.where(seat == slot, 1.0, 0.0).astype(jnp.bfloat16)
                weight[block, i] = jnp.broadcast_to(amount, shape)

    x = jnp.concatenate([r[...] for r in rows], axis=0)
    for block in range(count):
        for i in range(2):
            slots = jnp.dot(
                turned[block, i],
                x[block * BLOCK : (block + 1) * BLOCK],
                preferred_element_type=f32,
            )
            picked[i][block * SLOTS : (block + 1) * SLOTS] = slots.astype(jnp.bfloat16)


def pick(experts, pieces, after=()):
    sizes = tuple(p.shape[0] for p in pieces)
    blocks = sum(sizes) // BLOCK
    tile = 1792
    spec = pl.BlockSpec((blocks, 2, BLOCK, SLOTS), lambda i: (0, 0, 0, 0))
    out = pl.BlockSpec((blocks * SLOTS, tile), lambda i: (0, i))
    return pl.pallas_call(
        functools.partial(pick_kernel, sizes),
        grid=(D // tile,),
        in_specs=[pl.BlockSpec(memory_space=pltpu.SMEM)]
        + [pl.BlockSpec((n, BESIDE), lambda i: (0, D // BESIDE)) for n in sizes]
        + [pl.BlockSpec((n, tile), lambda i: (0, i)) for n in sizes]
        + [pl.BlockSpec(memory_space=pl.ANY) for _ in after],
        out_specs=[out, out, spec, spec],
        out_shape=[
            jax.ShapeDtypeStruct((blocks * SLOTS, D), jnp.bfloat16),
            jax.ShapeDtypeStruct((blocks * SLOTS, D), jnp.bfloat16),
            jax.ShapeDtypeStruct((blocks, 2, BLOCK, SLOTS), jnp.bfloat16),
            jax.ShapeDtypeStruct((blocks, 2, BLOCK, SLOTS), jnp.float32),
        ],
        scratch_shapes=[pltpu.VMEM((blocks, 2, SLOTS, BLOCK), jnp.bfloat16)],
        compiler_params=pltpu.CompilerParams(vmem_limit_bytes=40 * 2**20),
    )(experts, *pieces, *pieces, *after)


def experts_kernel(own, twin, gate, upward, down, own_out, twin_out, total):
    f32 = jnp.float32
    tile = pl.program_id(0)
    half = own.shape[0]

    @pl.when(tile == 0)
    def _():
        total[...] = jnp.zeros_like(total)

    x = jnp.concatenate([own[...], twin[...]], axis=0)
    g = jnp.dot(x, gate[0], preferred_element_type=f32)
    u = jnp.dot(x, upward[0], preferred_element_type=f32)
    inner = (g / (1.0 + jnp.exp(-g)) * u).astype(jnp.bfloat16)
    total[...] += jnp.dot(inner, down[0], preferred_element_type=f32)

    @pl.when(tile == pl.num_programs(0) - 1)
    def _():
        own_out[...] = total[:half].astype(jnp.bfloat16)
        twin_out[...] = total[half:].astype(jnp.bfloat16)


def run_experts(own, twin, gate, upward, down, tile=256):
    rows, hidden = own.shape[0], gate.shape[2]
    whole = pl.BlockSpec((rows, D), lambda i: (0, 0))
    return pl.pallas_call(
        experts_kernel,
        grid=(hidden // tile,),
        in_specs=[
            whole,
            whole,
            pl.BlockSpec((1, D, tile), lambda i: (0, 0, i)),
            pl.BlockSpec((1, D, tile), lambda i: (0, 0, i)),
            pl.BlockSpec((1, tile, D), lambda i: (0, i, 0)),
        ],
        out_specs=[whole, whole],
        out_shape=[jax.ShapeDtypeStruct((rows, D), jnp.bfloat16)] * 2,
        scratch_shapes=[pltpu.VMEM((2 * rows, D), jnp.float32)],
        compiler_params=pltpu.CompilerParams(vmem_limit_bytes=40 * 2**20),
        cost_estimate=pl.CostEstimate(flops=rows * D, bytes_accessed=rows * D, transcendentals=0),
    )(own, twin, gate, upward, down)


def spread_kernel(put, weight, own, twin, low, high):
    total = 0.0
    for i, half in enumerate((own, twin)):
        back = jnp.dot(put[0, i], half[...], preferred_element_type=jnp.float32)
        total = total + back * weight[0, i, :, :1]
    total = total.astype(jnp.bfloat16)
    low[...] = total[: BLOCK // 2]
    high[...] = total[BLOCK // 2 :]


def spread(put, weight, own, twin):
    tile = 1792
    table = pl.BlockSpec((1, 2, BLOCK, SLOTS), lambda i: (0, 0, 0, 0))
    columns = pl.BlockSpec((SLOTS, tile), lambda i: (0, i))
    return pl.pallas_call(
        spread_kernel,
        grid=(D // tile,),
        in_specs=[table, table, columns, columns],
        out_specs=[pl.BlockSpec((BLOCK // 2, tile), lambda i: (0, i))] * 2,
        out_shape=[jax.ShapeDtypeStruct((BLOCK // 2, D), jnp.bfloat16)] * 2,
        compiler_params=pltpu.CompilerParams(vmem_limit_bytes=40 * 2**20),
    )(put, weight, own, twin)


def other_core(x):
    return lax.ppermute(x, "ep", OTHER_CORE)


def exchange(x):
    return lax.all_to_all(x, "ep", 0, 0, tiled=True, axis_index_groups=SAME_CORE)


def attend_kernel(lengths, queries, keys, rotary_keys, mixed):
    f32 = jnp.float32
    scale = 1.0 / (NOPE + ROPE) ** 0.5
    shape = (CHIPS * HC * STEPS, KEYS)
    step, place = lax.broadcasted_iota(jnp.int32, shape, 0) % STEPS, lax.broadcasted_iota(jnp.int32, shape, 1)
    known = (place >= LMAX) & (place - LMAX <= step)
    for row in range(ROWS_DEV):
        query = queries[:, row].reshape(shape[0], LAT + ROPE)
        key = keys[row]
        score = lax.dot_general(
            query[:, :LAT], key, (((1,), (1,)), ((), ())), preferred_element_type=f32
        )
        score = score + jnp.dot(query[:, LAT:], rotary_keys[row], preferred_element_type=f32)
        live = known | ((place < LMAX) & (place < lengths[row]))
        score = jnp.where(live, score * scale, -jnp.inf)
        prob = jnp.exp(score - jnp.max(score, axis=1, keepdims=True))
        prob = (prob / jnp.sum(prob, axis=1, keepdims=True)).astype(jnp.bfloat16)
        out = jnp.dot(prob, key, preferred_element_type=f32).astype(jnp.bfloat16)
        mixed[:, row] = out.reshape(CHIPS, HC * STEPS, LAT)


def attend(queries, cache_latent, cache_rotary, lengths, new_latent, new_rotary):
    spare = KEYS - LMAX - STEPS
    keys = jnp.concatenate([cache_latent, jnp.swapaxes(new_latent, 0, 1)], axis=1)
    keys = jnp.pad(keys, ((0, 0), (0, spare), (0, 0)))
    rotary_keys = jnp.concatenate([cache_rotary, jnp.transpose(new_rotary, (1, 2, 0))], axis=2)
    rotary_keys = jnp.pad(rotary_keys, ((0, 0), (0, 0), (0, spare)))
    return pl.pallas_call(
        attend_kernel,
        in_specs=[pl.BlockSpec(memory_space=pltpu.SMEM)]
        + [pl.BlockSpec(memory_space=pltpu.VMEM)] * 3,
        out_specs=pl.BlockSpec(memory_space=pltpu.VMEM),
        out_shape=jax.ShapeDtypeStruct((CHIPS, ROWS_DEV, HC * STEPS, LAT), jnp.bfloat16),
        compiler_params=pltpu.CompilerParams(vmem_limit_bytes=40 * 2**20),
    )(lengths, queries, keys, rotary_keys)


def per_device(
    query_plain,
    query_rotary,
    key_up,
    value_up,
    output_weight,
    cache_latent,
    cache_rotary,
    lengths,
    new_latent,
    new_rotary,
    residual,
    norm_gain,
    expert_ids,
    gate_weights,
    expert_gate,
    expert_up,
    expert_down,
):
    f32 = jnp.float32
    bf16 = jnp.bfloat16
    core = lax.axis_index("ep") % 2
    expert = lax.axis_index("dp") * lax.axis_size("ep") + lax.axis_index("ep")

    queries = jnp.concatenate([query_plain, query_rotary], axis=2)
    queries = queries.reshape(STEPS, CHIPS, 2, ROWS_DEV, 2 * (NOPE + ROPE))
    kept = lax.dynamic_index_in_dim(queries, core, axis=2, keepdims=False)
    given = lax.dynamic_index_in_dim(queries, 1 - core, axis=2, keepdims=False)
    given = other_core(given)
    key_map = jnp.concatenate([key_up, other_core(key_up)], axis=0)
    value_map = jnp.concatenate([value_up, other_core(value_up)], axis=0)
    out_map = jnp.concatenate([output_weight, other_core(output_weight)], axis=0)
    split = 2 * NOPE
    plain = jnp.stack([kept[..., :split], given[..., :split]], axis=3)
    plain = plain.reshape(STEPS, CHIPS, ROWS_DEV, HC, NOPE)
    rotary = jnp.stack([kept[..., split:], given[..., split:]], axis=3)
    rotary = rotary.reshape(STEPS, CHIPS, ROWS_DEV, HC, ROPE)
    absorbed = jnp.einsum("sclhn,hnd->clhsd", plain, key_map, preferred_element_type=f32)
    absorbed = absorbed.astype(bf16).reshape(CHIPS, ROWS_DEV, HC * STEPS, LAT)
    rotary = jnp.transpose(rotary, (1, 2, 3, 0, 4)).reshape(CHIPS, ROWS_DEV, HC * STEPS, ROPE)
    sent = exchange(jnp.concatenate([absorbed, rotary], axis=3))
    mixed = attend(sent, cache_latent, cache_rotary, lengths, new_latent, new_rotary)
    mixed = exchange(mixed).reshape(CHIPS, ROWS_DEV, HC, STEPS, LAT)
    values = jnp.einsum("clhsd,hdv->clshv", mixed, value_map, preferred_element_type=f32)
    values = values.astype(bf16).reshape(CHIPS * RS, HC * VHEAD)
    parts = jnp.dot(values, out_map, preferred_element_type=f32).astype(bf16)
    parts = exchange(parts.reshape(CHIPS, RS, D))
    attention = jnp.sum(parts.astype(f32), axis=0)
    hidden = jnp.swapaxes(residual, 0, 1).reshape(RS, D).astype(f32) + attention
    normed = (
        hidden * lax.rsqrt(jnp.mean(hidden * hidden, axis=-1, keepdims=True) + 1e-06) * norm_gain
    ).astype(bf16)

    pair = jnp.stack([expert, expert ^ 1])

    streamed = [
        pltpu.with_memory_space_constraint(w, pltpu.HBM)
        for w in (expert_gate, expert_up, expert_down)
    ]

    def experts(own, twin):
        return run_experts(own, other_core(twin), *streamed)

    def work(pieces, after=()):
        own, twin, put, weight = pick(pair, pieces, after)
        own, twin = experts(own, twin)
        return own, spread(put, weight, own, other_core(twin))

    rows = jnp.concatenate([normed, routing(expert_ids, gate_weights)], axis=1)
    rows = plane_exchange(jnp.broadcast_to(rows[None], (16, RS, D + BESIDE)))
    rows = rows.reshape(BLOCK, D + BESIDE)
    half = BLOCK // 2
    low, high = rows[:half], rows[half:]
    before_low, after_high = shift(low, 0, 1), shift(high, 0, -1)
    before_high, after_low = shift(high, 0, 1), shift(low, 0, -1)
    far = [shift(before_low, 0, 1), shift(after_high, 0, -1)]

    result, (first_low, first_high) = work([before_low, after_high])
    result, (near_low, near_high) = work([after_low, before_high], [result])
    result, (far_low, far_high) = work(far, [result, first_low])
    first_low, first_high = shift(first_low, 0, -1), shift(first_high, 0, 1)
    far_low, far_high = shift(far_low, 0, 1), shift(far_high, 0, -1)
    near_low, near_high = shift(near_low + far_low, 0, 1), shift(near_high + far_high, 0, -1)
    _, (low, high) = work([rows], [result, first_low, first_high])
    total = [
        sum(x.astype(f32) for x in parts).astype(bf16)
        for parts in ((low, first_low, near_low), (high, first_high, near_high))
    ]
    total = jnp.concatenate(total, axis=0)
    routed = plane_exchange(total.reshape(16, RS, D))
    out = (hidden + jnp.sum(routed.astype(f32), axis=0)).astype(bf16)
    return jnp.swapaxes(out.reshape(ROWS_DEV, STEPS, D), 0, 1)


def solution(mesh):
    return jax.shard_map(
        per_device,
        mesh=mesh,
        in_specs=(
            P(None, "dp", "ep"),
            P(None, "dp", "ep"),
            P("ep", None, None),
            P("ep", None, None),
            P("ep", None),
            P(("dp", "ep"), None, None),
            P(("dp", "ep"), None, None),
            P(("dp", "ep")),
            P(None, ("dp", "ep"), None),
            P(None, ("dp", "ep"), None),
            P(None, ("dp", "ep"), None),
            P(),
            P(None, ("dp", "ep"), None),
            P(None, ("dp", "ep"), None),
            P(("dp", "ep"), None, None),
            P(("dp", "ep"), None, None),
            P(("dp", "ep"), None, None),
        ),
        out_specs=P(None, ("dp", "ep"), None),
        check_vma=False,
    )
```

```python
import functools

import jax
import jax.numpy as jnp
import numpy as np
from jax import lax
from jax.experimental import pallas as pl
from jax.experimental.pallas import tpu as pltpu
from jax.sharding import PartitionSpec as P

D = 3584
HEADS = 64
LAT = 512
ROPE = 64
NOPE = 128
VHEAD = 128
MOST = 2
TOP = 8
BLOCK = 256
SLOTS = 128
BESIDE = 128
STEPS = 4
EXPERTS = 128
LMAX = 64
KEYS = 128
ROWS_DEV = 4
CHIPS = 16
HC = 4
RS = STEPS * ROWS_DEV

SAME_CORE = [[2 * chip + core for chip in range(CHIPS)] for core in range(2)]
OTHER_CORE = [(i, i ^ 1) for i in range(2 * CHIPS)]
PLANES = [
    [y * 32 + first * unit + second * (10 - unit) + core for second in range(4) for y in range(4)]
    for core, unit in ((0, 8), (1, 2))
    for first in range(4)
]


SEATS = MOST * STEPS


def place_of(axis):
    group = lax.axis_index("ep")
    return {"y": lax.axis_index("dp"), "x": group // 8, "z": group // 2 % 4}[axis]


def shift(x, turn, by):
    if turn == 2:
        return lax.ppermute(x, "dp", [(i, (i + by) % 4) for i in range(4)])
    pairs = []
    for i in range(2 * CHIPS):
        unit = 8 if i % 2 == turn else 2
        pairs.append((i, i + ((i // unit + by) % 4 - i // unit % 4) * unit))
    return lax.ppermute(x, "ep", pairs)


def plane_exchange(x):
    return lax.all_to_all(x, ("dp", "ep"), 0, 0, tiled=True, axis_index_groups=PLANES)


def routing(expert_ids, gate_weights):
    ids = jnp.swapaxes(expert_ids, 0, 1).reshape(RS, -1).astype(jnp.float32)
    rest = jnp.swapaxes(gate_weights, 0, 1).reshape(RS, -1)
    columns = [ids]
    for _ in range(3):
        columns.append(lax.reduce_precision(rest, 8, 7))
        rest = rest - columns[-1]
    columns = jnp.concatenate(columns, axis=1)
    return jnp.pad(columns, ((0, 0), (0, BESIDE - columns.shape[1]))).astype(jnp.bfloat16)


def pick_kernel(pieces, experts, *refs):
    f32 = jnp.float32
    count = sum(pieces) // BLOCK
    columns, rows = refs[: len(pieces)], refs[len(pieces) : 2 * len(pieces)]
    *picked, put, weight, turned = refs[-5:]

    @pl.when(pl.program_id(0) == 0)
    def _():
        shape = (BLOCK, BLOCK)
        this, other = (lax.broadcasted_iota(jnp.int32, shape, i) for i in (0, 1))
        earlier = (
            (this // RS == other // RS)
            & (this % STEPS == other % STEPS)
            & (this % RS // STEPS > other % RS // STEPS)
        ).astype(jnp.bfloat16)
        shape = (BLOCK, BESIDE)
        row, lane = (lax.broadcasted_iota(jnp.int32, shape, i) for i in (0, 1))
        base = (row // RS * SEATS + row % STEPS * MOST).astype(f32)
        beside = jnp.concatenate([c[...] for c in columns], axis=0).astype(f32)
        for block in range(count):
            ids = beside[block * BLOCK : (block + 1) * BLOCK]
            weights = sum(pltpu.roll(ids, BESIDE - i * TOP, 1) for i in (1, 2, 3))
            for i in range(2):
                same = (ids == experts[i].astype(f32)) & (lane < TOP)
                amount = jnp.sum(jnp.where(same, weights, 0.0), axis=1, keepdims=True)
                named = jnp.max(jnp.where(same, 1.0, 0.0), axis=1, keepdims=True)
                named = jnp.broadcast_to(named, shape)
                rank = jnp.dot(earlier, named.astype(jnp.bfloat16), preferred_element_type=f32)
                seat = jnp.where(named > 0.0, rank + base, -1.0)
                put[block, i] = jnp.where(seat == lane.astype(f32), 1.0, 0.0).astype(jnp.bfloat16)
                seat = jnp.transpose(seat)
                slot = lax.broadcasted_iota(jnp.int32, seat.shape, 0).astype(f32)
                turned[block, i] = jnp.where(seat == slot, 1.0, 0.0).astype(jnp.bfloat16)
                weight[block, i] = jnp.broadcast_to(amount, shape)

    x = jnp.concatenate([r[...] for r in rows], axis=0)
    for block in range(count):
        for i in range(2):
            slots = jnp.dot(
                turned[block, i],
                x[block * BLOCK : (block + 1) * BLOCK],
                preferred_element_type=f32,
            )
            picked[i][block * SLOTS : (block + 1) * SLOTS] = slots.astype(jnp.bfloat16)


def pick(experts, pieces, after=()):
    sizes = tuple(p.shape[0] for p in pieces)
    blocks = sum(sizes) // BLOCK
    tile = 1792
    spec = pl.BlockSpec((blocks, 2, BLOCK, SLOTS), lambda i: (0, 0, 0, 0))
    out = pl.BlockSpec((blocks * SLOTS, tile), lambda i: (0, i))
    return pl.pallas_call(
        functools.partial(pick_kernel, sizes),
        grid=(D // tile,),
        in_specs=[pl.BlockSpec(memory_space=pltpu.SMEM)]
        + [pl.BlockSpec((n, BESIDE), lambda i: (0, D // BESIDE)) for n in sizes]
        + [pl.BlockSpec((n, tile), lambda i: (0, i)) for n in sizes]
        + [pl.BlockSpec(memory_space=pl.ANY) for _ in after],
        out_specs=[out, out, spec, spec],
        out_shape=[
            jax.ShapeDtypeStruct((blocks * SLOTS, D), jnp.bfloat16),
            jax.ShapeDtypeStruct((blocks * SLOTS, D), jnp.bfloat16),
            jax.ShapeDtypeStruct((blocks, 2, BLOCK, SLOTS), jnp.bfloat16),
            jax.ShapeDtypeStruct((blocks, 2, BLOCK, SLOTS), jnp.float32),
        ],
        scratch_shapes=[pltpu.VMEM((blocks, 2, SLOTS, BLOCK), jnp.bfloat16)],
        compiler_params=pltpu.CompilerParams(vmem_limit_bytes=10 * 2**20),
    )(experts, *pieces, *pieces, *after)


def experts_kernel(own, twin, gate, upward, down, own_out, twin_out, total):
    f32 = jnp.float32
    tile = pl.program_id(0)
    half = own.shape[0]

    @pl.when(tile == 0)
    def _():
        total[...] = jnp.zeros_like(total)

    x = jnp.concatenate([own[...], twin[...]], axis=0)
    columns = pl.ds(pl.multiple_of(tile * down.shape[1], down.shape[1]), down.shape[1])
    g = jnp.dot(x, gate[0, :, columns], preferred_element_type=f32)
    u = jnp.dot(x, upward[0], preferred_element_type=f32)
    inner = (g / (1.0 + jnp.exp(-g)) * u).astype(jnp.bfloat16)
    total[...] += jnp.dot(inner, down[0], preferred_element_type=f32)

    @pl.when(tile == pl.num_programs(0) - 1)
    def _():
        own_out[...] = total[:half].astype(jnp.bfloat16)
        twin_out[...] = total[half:].astype(jnp.bfloat16)


def run_experts(own, twin, gate, upward, down, tile=256):
    rows, hidden = own.shape[0], gate.shape[2]
    whole = pl.BlockSpec((rows, D), lambda i: (0, 0))
    return pl.pallas_call(
        experts_kernel,
        grid=(hidden // tile,),
        in_specs=[
            whole,
            whole,
            pl.BlockSpec(memory_space=pltpu.VMEM),
            pl.BlockSpec((1, D, tile), lambda i: (0, 0, i)),
            pl.BlockSpec((1, tile, D), lambda i: (0, i, 0)),
        ],
        out_specs=[whole, whole],
        out_shape=[jax.ShapeDtypeStruct((rows, D), jnp.bfloat16)] * 2,
        scratch_shapes=[pltpu.VMEM((2 * rows, D), jnp.float32)],
        compiler_params=pltpu.CompilerParams(vmem_limit_bytes=24 * 2**20),
        cost_estimate=pl.CostEstimate(flops=rows * D, bytes_accessed=rows * D, transcendentals=0),
    )(own, twin, gate, upward, down)


def mark_kernel(*refs):
    refs[-1][...] = jnp.zeros_like(refs[-1])


def mark(*arrays):
    return pl.pallas_call(
        mark_kernel,
        in_specs=[pl.BlockSpec(memory_space=pl.ANY) for _ in arrays],
        out_shape=jax.ShapeDtypeStruct((8, 128), jnp.float32),
        compiler_params=pltpu.CompilerParams(vmem_limit_bytes=2**20),
    )(*arrays)


def spread_kernel(put, weight, own, twin, low, high):
    total = 0.0
    for i, half in enumerate((own, twin)):
        back = jnp.dot(put[0, i], half[...], preferred_element_type=jnp.float32)
        total = total + back * weight[0, i, :, :1]
    total = total.astype(jnp.bfloat16)
    low[...] = total[: BLOCK // 2]
    high[...] = total[BLOCK // 2 :]


def spread(put, weight, own, twin):
    tile = 1792
    table = pl.BlockSpec((1, 2, BLOCK, SLOTS), lambda i: (0, 0, 0, 0))
    columns = pl.BlockSpec((SLOTS, tile), lambda i: (0, i))
    return pl.pallas_call(
        spread_kernel,
        grid=(D // tile,),
        in_specs=[table, table, columns, columns],
        out_specs=[pl.BlockSpec((BLOCK // 2, tile), lambda i: (0, i))] * 2,
        out_shape=[jax.ShapeDtypeStruct((BLOCK // 2, D), jnp.bfloat16)] * 2,
        compiler_params=pltpu.CompilerParams(vmem_limit_bytes=10 * 2**20),
    )(put, weight, own, twin)


def other_core(x):
    return lax.ppermute(x, "ep", OTHER_CORE)


def exchange(x):
    return lax.all_to_all(x, "ep", 0, 0, tiled=True, axis_index_groups=SAME_CORE)


def attend_kernel(lengths, queries, keys, rotary_keys, mixed):
    f32 = jnp.float32
    scale = 1.0 / (NOPE + ROPE) ** 0.5
    shape = (CHIPS * HC * STEPS, KEYS)
    step, place = lax.broadcasted_iota(jnp.int32, shape, 0) % STEPS, lax.broadcasted_iota(jnp.int32, shape, 1)
    known = (place >= LMAX) & (place - LMAX <= step)
    for row in range(ROWS_DEV):
        query = queries[:, row].reshape(shape[0], LAT + ROPE)
        key = keys[row]
        score = lax.dot_general(
            query[:, :LAT], key, (((1,), (1,)), ((), ())), preferred_element_type=f32
        )
        score = score + jnp.dot(query[:, LAT:], rotary_keys[row], preferred_element_type=f32)
        live = known | ((place < LMAX) & (place < lengths[row]))
        score = jnp.where(live, score * scale, -jnp.inf)
        prob = jnp.exp(score - jnp.max(score, axis=1, keepdims=True))
        prob = (prob / jnp.sum(prob, axis=1, keepdims=True)).astype(jnp.bfloat16)
        out = jnp.dot(prob, key, preferred_element_type=f32).astype(jnp.bfloat16)
        mixed[:, row] = out.reshape(CHIPS, HC * STEPS, LAT)


def attend(queries, cache_latent, cache_rotary, lengths, new_latent, new_rotary):
    spare = KEYS - LMAX - STEPS
    keys = jnp.concatenate([cache_latent, jnp.swapaxes(new_latent, 0, 1)], axis=1)
    keys = jnp.pad(keys, ((0, 0), (0, spare), (0, 0)))
    rotary_keys = jnp.concatenate([cache_rotary, jnp.transpose(new_rotary, (1, 2, 0))], axis=2)
    rotary_keys = jnp.pad(rotary_keys, ((0, 0), (0, 0), (0, spare)))
    return pl.pallas_call(
        attend_kernel,
        in_specs=[pl.BlockSpec(memory_space=pltpu.SMEM)]
        + [pl.BlockSpec(memory_space=pltpu.VMEM)] * 3,
        out_specs=pl.BlockSpec(memory_space=pltpu.VMEM),
        out_shape=jax.ShapeDtypeStruct((CHIPS, ROWS_DEV, HC * STEPS, LAT), jnp.bfloat16),
        compiler_params=pltpu.CompilerParams(vmem_limit_bytes=16 * 2**20),
    )(lengths, queries, keys, rotary_keys)


def per_device(
    query_plain,
    query_rotary,
    key_up,
    value_up,
    output_weight,
    cache_latent,
    cache_rotary,
    lengths,
    new_latent,
    new_rotary,
    residual,
    norm_gain,
    expert_ids,
    gate_weights,
    expert_gate,
    expert_up,
    expert_down,
):
    f32 = jnp.float32
    bf16 = jnp.bfloat16
    core = lax.axis_index("ep") % 2
    expert = lax.axis_index("dp") * lax.axis_size("ep") + lax.axis_index("ep")

    queries = jnp.concatenate([query_plain, query_rotary], axis=2)
    queries = queries.reshape(STEPS, CHIPS, 2, ROWS_DEV, 2 * (NOPE + ROPE))
    kept = lax.dynamic_index_in_dim(queries, core, axis=2, keepdims=False)
    given = lax.dynamic_index_in_dim(queries, 1 - core, axis=2, keepdims=False)
    given = other_core(given)
    key_map = jnp.concatenate([key_up, other_core(key_up)], axis=0)
    value_map = jnp.concatenate([value_up, other_core(value_up)], axis=0)
    out_map = jnp.concatenate([output_weight, other_core(output_weight)], axis=0)
    split = 2 * NOPE
    plain = jnp.stack([kept[..., :split], given[..., :split]], axis=3)
    plain = plain.reshape(STEPS, CHIPS, ROWS_DEV, HC, NOPE)
    rotary = jnp.stack([kept[..., split:], given[..., split:]], axis=3)
    rotary = rotary.reshape(STEPS, CHIPS, ROWS_DEV, HC, ROPE)
    absorbed = jnp.einsum("sclhn,hnd->clhsd", plain, key_map, preferred_element_type=f32)
    absorbed = absorbed.astype(bf16).reshape(CHIPS, ROWS_DEV, HC * STEPS, LAT)
    rotary = jnp.transpose(rotary, (1, 2, 3, 0, 4)).reshape(CHIPS, ROWS_DEV, HC * STEPS, ROPE)
    sent = exchange(jnp.concatenate([absorbed, rotary], axis=3))
    mixed = attend(sent, cache_latent, cache_rotary, lengths, new_latent, new_rotary)
    mixed = exchange(mixed).reshape(CHIPS, ROWS_DEV, HC, STEPS, LAT)
    values = jnp.einsum("clhsd,hdv->clshv", mixed, value_map, preferred_element_type=f32)
    values = values.astype(bf16).reshape(CHIPS * RS, HC * VHEAD)
    parts = jnp.dot(values, out_map, preferred_element_type=f32).astype(bf16)
    parts = exchange(parts.reshape(CHIPS, RS, D))
    attention = jnp.sum(parts.astype(f32), axis=0)
    hidden = jnp.swapaxes(residual, 0, 1).reshape(RS, D).astype(f32) + attention
    normed = (
        hidden * lax.rsqrt(jnp.mean(hidden * hidden, axis=-1, keepdims=True) + 1e-06) * norm_gain
    ).astype(bf16)

    pair = jnp.stack([expert, expert ^ 1])

    weights = [
        pltpu.with_memory_space_constraint(w, place)
        for w, place in (
            (expert_gate, pltpu.VMEM),
            (expert_up, pltpu.HBM),
            (expert_down, pltpu.HBM),
        )
    ]

    def experts(own, twin):
        return run_experts(own, other_core(twin), *weights)

    def work(pieces, after=()):
        own, twin, put, weight = pick(pair, pieces, after)
        own, twin = experts(own, twin)
        return own, spread(put, weight, own, other_core(twin))

    rows = jnp.concatenate([normed, routing(expert_ids, gate_weights)], axis=1)
    rows = plane_exchange(jnp.broadcast_to(rows[None], (16, RS, D + BESIDE)))
    rows = rows.reshape(BLOCK, D + BESIDE)
    half = BLOCK // 2
    low, high = rows[:half], rows[half:]
    before_low, after_high = shift(low, 0, 1), shift(high, 0, -1)
    before_high, after_low = shift(high, 0, 1), shift(low, 0, -1)
    far = [shift(before_low, 0, 1), shift(after_high, 0, -1)]

    here = mark(rows[:16, :128], weights[0])
    result, (first_low, first_high) = work([before_low, after_high], [here])
    result, (near_low, near_high) = work([after_low, before_high], [result])
    result, (far_low, far_high) = work(far, [result, first_low])
    first_low, first_high = shift(first_low, 0, -1), shift(first_high, 0, 1)
    far_low, far_high = shift(far_low, 0, 1), shift(far_high, 0, -1)
    near_low, near_high = shift(near_low + far_low, 0, 1), shift(near_high + far_high, 0, -1)
    _, (low, high) = work([rows], [result, first_low, first_high])
    total = [
        sum(x.astype(f32) for x in parts).astype(bf16)
        for parts in ((low, first_low, near_low), (high, first_high, near_high))
    ]
    total = jnp.concatenate(total, axis=0)
    routed = plane_exchange(total.reshape(16, RS, D))
    out = (hidden + jnp.sum(routed.astype(f32), axis=0)).astype(bf16)
    return jnp.swapaxes(out.reshape(ROWS_DEV, STEPS, D), 0, 1)


def solution(mesh):
    return jax.shard_map(
        per_device,
        mesh=mesh,
        in_specs=(
            P(None, "dp", "ep"),
            P(None, "dp", "ep"),
            P("ep", None, None),
            P("ep", None, None),
            P("ep", None),
            P(("dp", "ep"), None, None),
            P(("dp", "ep"), None, None),
            P(("dp", "ep")),
            P(None, ("dp", "ep"), None),
            P(None, ("dp", "ep"), None),
            P(None, ("dp", "ep"), None),
            P(),
            P(None, ("dp", "ep"), None),
            P(None, ("dp", "ep"), None),
            P(("dp", "ep"), None, None),
            P(("dp", "ep"), None, None),
            P(("dp", "ep"), None, None),
        ),
        out_specs=P(None, ("dp", "ep"), None),
        check_vma=False,
    )
```

```python
import functools

import jax
import jax.numpy as jnp
import numpy as np
from jax import lax
from jax.experimental import pallas as pl
from jax.experimental.pallas import tpu as pltpu
from jax.sharding import PartitionSpec as P

D = 3584
HEADS = 64
LAT = 512
ROPE = 64
NOPE = 128
VHEAD = 128
MOST = 2
TOP = 8
BLOCK = 256
SLOTS = 128
BESIDE = 128
STEPS = 4
EXPERTS = 128
LMAX = 64
KEYS = 128
ROWS_DEV = 4
CHIPS = 16
HC = 4
RS = STEPS * ROWS_DEV

SAME_CORE = [[2 * chip + core for chip in range(CHIPS)] for core in range(2)]
OTHER_CORE = [(i, i ^ 1) for i in range(2 * CHIPS)]
PLANES = [
    [y * 32 + first * unit + second * (10 - unit) + core for second in range(4) for y in range(4)]
    for core, unit in ((0, 8), (1, 2))
    for first in range(4)
]


SEATS = MOST * STEPS


def place_of(axis):
    group = lax.axis_index("ep")
    return {"y": lax.axis_index("dp"), "x": group // 8, "z": group // 2 % 4}[axis]


def shift(x, turn, by):
    if turn == 2:
        return lax.ppermute(x, "dp", [(i, (i + by) % 4) for i in range(4)])
    pairs = []
    for i in range(2 * CHIPS):
        unit = 8 if i % 2 == turn else 2
        pairs.append((i, i + ((i // unit + by) % 4 - i // unit % 4) * unit))
    return lax.ppermute(x, "ep", pairs)


def plane_exchange(x):
    return lax.all_to_all(x, ("dp", "ep"), 0, 0, tiled=True, axis_index_groups=PLANES)


def routing(expert_ids, gate_weights):
    ids = jnp.swapaxes(expert_ids, 0, 1).reshape(RS, -1).astype(jnp.float32)
    rest = jnp.swapaxes(gate_weights, 0, 1).reshape(RS, -1)
    columns = [ids]
    for _ in range(3):
        columns.append(lax.reduce_precision(rest, 8, 7))
        rest = rest - columns[-1]
    columns = jnp.concatenate(columns, axis=1)
    return jnp.pad(columns, ((0, 0), (0, BESIDE - columns.shape[1]))).astype(jnp.bfloat16)


def pick_kernel(pieces, experts, *refs):
    f32 = jnp.float32
    count = sum(pieces) // BLOCK
    columns, rows = refs[: len(pieces)], refs[len(pieces) : 2 * len(pieces)]
    *picked, put, weight, turned = refs[-5:]

    @pl.when(pl.program_id(0) == 0)
    def _():
        shape = (BLOCK, BLOCK)
        this, other = (lax.broadcasted_iota(jnp.int32, shape, i) for i in (0, 1))
        earlier = (
            (this // RS == other // RS)
            & (this % STEPS == other % STEPS)
            & (this % RS // STEPS > other % RS // STEPS)
        ).astype(jnp.bfloat16)
        shape = (BLOCK, BESIDE)
        row, lane = (lax.broadcasted_iota(jnp.int32, shape, i) for i in (0, 1))
        base = (row // RS * SEATS + row % STEPS * MOST).astype(f32)
        beside = jnp.concatenate([c[...] for c in columns], axis=0).astype(f32)
        for block in range(count):
            ids = beside[block * BLOCK : (block + 1) * BLOCK]
            weights = sum(pltpu.roll(ids, BESIDE - i * TOP, 1) for i in (1, 2, 3))
            for i in range(2):
                same = (ids == experts[i].astype(f32)) & (lane < TOP)
                amount = jnp.sum(jnp.where(same, weights, 0.0), axis=1, keepdims=True)
                named = jnp.max(jnp.where(same, 1.0, 0.0), axis=1, keepdims=True)
                named = jnp.broadcast_to(named, shape)
                rank = jnp.dot(earlier, named.astype(jnp.bfloat16), preferred_element_type=f32)
                seat = jnp.where(named > 0.0, rank + base, -1.0)
                put[block, i] = jnp.where(seat == lane.astype(f32), 1.0, 0.0).astype(jnp.bfloat16)
                seat = jnp.transpose(seat)
                slot = lax.broadcasted_iota(jnp.int32, seat.shape, 0).astype(f32)
                turned[block, i] = jnp.where(seat == slot, 1.0, 0.0).astype(jnp.bfloat16)
                weight[block, i] = jnp.broadcast_to(amount, shape)

    x = jnp.concatenate([r[...] for r in rows], axis=0)
    for block in range(count):
        for i in range(2):
            slots = jnp.dot(
                turned[block, i],
                x[block * BLOCK : (block + 1) * BLOCK],
                preferred_element_type=f32,
            )
            picked[i][block * SLOTS : (block + 1) * SLOTS] = slots.astype(jnp.bfloat16)


def pick(experts, pieces, after=()):
    sizes = tuple(p.shape[0] for p in pieces)
    blocks = sum(sizes) // BLOCK
    tile = D
    spec = pl.BlockSpec((blocks, 2, BLOCK, SLOTS), lambda i: (0, 0, 0, 0))
    out = pl.BlockSpec((blocks * SLOTS, tile), lambda i: (0, i))
    return pl.pallas_call(
        functools.partial(pick_kernel, sizes),
        grid=(D // tile,),
        in_specs=[pl.BlockSpec(memory_space=pltpu.SMEM)]
        + [pl.BlockSpec((n, BESIDE), lambda i: (0, D // BESIDE)) for n in sizes]
        + [pl.BlockSpec((n, tile), lambda i: (0, i)) for n in sizes]
        + [pl.BlockSpec(memory_space=pl.ANY) for _ in after],
        out_specs=[out, out, spec, spec],
        out_shape=[
            jax.ShapeDtypeStruct((blocks * SLOTS, D), jnp.bfloat16),
            jax.ShapeDtypeStruct((blocks * SLOTS, D), jnp.bfloat16),
            jax.ShapeDtypeStruct((blocks, 2, BLOCK, SLOTS), jnp.bfloat16),
            jax.ShapeDtypeStruct((blocks, 2, BLOCK, SLOTS), jnp.float32),
        ],
        scratch_shapes=[pltpu.VMEM((blocks, 2, SLOTS, BLOCK), jnp.bfloat16)],
        compiler_params=pltpu.CompilerParams(vmem_limit_bytes=14 * 2**20),
    )(experts, *pieces, *pieces, *after)


def experts_kernel(own, twin, gate, upward, down, own_out, twin_out, total):
    f32 = jnp.float32
    tile = pl.program_id(0)
    half = own.shape[0]

    @pl.when(tile == 0)
    def _():
        total[...] = jnp.zeros_like(total)

    x = jnp.concatenate([own[...], twin[...]], axis=0)
    columns = pl.ds(pl.multiple_of(tile * down.shape[1], down.shape[1]), down.shape[1])
    g = jnp.dot(x, gate[0, :, columns], preferred_element_type=f32)
    u = jnp.dot(x, upward[0], preferred_element_type=f32)
    inner = (g / (1.0 + jnp.exp(-g)) * u).astype(jnp.bfloat16)
    total[...] += jnp.dot(inner, down[0], preferred_element_type=f32)

    @pl.when(tile == pl.num_programs(0) - 1)
    def _():
        own_out[...] = total[:half].astype(jnp.bfloat16)
        twin_out[...] = total[half:].astype(jnp.bfloat16)


def run_experts(own, twin, gate, upward, down, tile=256):
    rows, hidden = own.shape[0], gate.shape[2]
    whole = pl.BlockSpec((rows, D), lambda i: (0, 0))
    return pl.pallas_call(
        experts_kernel,
        grid=(hidden // tile,),
        in_specs=[
            whole,
            whole,
            pl.BlockSpec(memory_space=pltpu.VMEM),
            pl.BlockSpec((1, D, tile), lambda i: (0, 0, i)),
            pl.BlockSpec((1, tile, D), lambda i: (0, i, 0)),
        ],
        out_specs=[whole, whole],
        out_shape=[jax.ShapeDtypeStruct((rows, D), jnp.bfloat16)] * 2,
        scratch_shapes=[pltpu.VMEM((2 * rows, D), jnp.float32)],
        compiler_params=pltpu.CompilerParams(vmem_limit_bytes=24 * 2**20),
        cost_estimate=pl.CostEstimate(flops=rows * D, bytes_accessed=rows * D, transcendentals=0),
    )(own, twin, gate, upward, down)


def mark_kernel(*refs):
    refs[-1][...] = jnp.zeros_like(refs[-1])


def mark(*arrays):
    return pl.pallas_call(
        mark_kernel,
        in_specs=[pl.BlockSpec(memory_space=pl.ANY) for _ in arrays],
        out_shape=jax.ShapeDtypeStruct((8, 128), jnp.float32),
        compiler_params=pltpu.CompilerParams(vmem_limit_bytes=2**20),
    )(*arrays)


def spread_kernel(put, weight, own, twin, low, high):
    total = 0.0
    for i, half in enumerate((own, twin)):
        back = jnp.dot(put[0, i], half[...], preferred_element_type=jnp.float32)
        total = total + back * weight[0, i, :, :1]
    total = total.astype(jnp.bfloat16)
    low[...] = total[: BLOCK // 2]
    high[...] = total[BLOCK // 2 :]


def spread(put, weight, own, twin):
    tile = D
    table = pl.BlockSpec((1, 2, BLOCK, SLOTS), lambda i: (0, 0, 0, 0))
    columns = pl.BlockSpec((SLOTS, tile), lambda i: (0, i))
    return pl.pallas_call(
        spread_kernel,
        grid=(D // tile,),
        in_specs=[table, table, columns, columns],
        out_specs=[pl.BlockSpec((BLOCK // 2, tile), lambda i: (0, i))] * 2,
        out_shape=[jax.ShapeDtypeStruct((BLOCK // 2, D), jnp.bfloat16)] * 2,
        compiler_params=pltpu.CompilerParams(vmem_limit_bytes=14 * 2**20),
    )(put, weight, own, twin)


def other_core(x):
    return lax.ppermute(x, "ep", OTHER_CORE)


def exchange(x):
    return lax.all_to_all(x, "ep", 0, 0, tiled=True, axis_index_groups=SAME_CORE)


def attend_kernel(lengths, queries, keys, rotary_keys, mixed):
    f32 = jnp.float32
    scale = 1.0 / (NOPE + ROPE) ** 0.5
    shape = (CHIPS * HC * STEPS, KEYS)
    step, place = lax.broadcasted_iota(jnp.int32, shape, 0) % STEPS, lax.broadcasted_iota(jnp.int32, shape, 1)
    known = (place >= LMAX) & (place - LMAX <= step)
    for row in range(ROWS_DEV):
        query = queries[:, row].reshape(shape[0], LAT + ROPE)
        key = keys[row]
        score = lax.dot_general(
            query[:, :LAT], key, (((1,), (1,)), ((), ())), preferred_element_type=f32
        )
        score = score + jnp.dot(query[:, LAT:], rotary_keys[row], preferred_element_type=f32)
        live = known | ((place < LMAX) & (place < lengths[row]))
        score = jnp.where(live, score * scale, -jnp.inf)
        prob = jnp.exp(score - jnp.max(score, axis=1, keepdims=True))
        prob = (prob / jnp.sum(prob, axis=1, keepdims=True)).astype(jnp.bfloat16)
        out = jnp.dot(prob, key, preferred_element_type=f32).astype(jnp.bfloat16)
        mixed[:, row] = out.reshape(CHIPS, HC * STEPS, LAT)


def attend(queries, cache_latent, cache_rotary, lengths, new_latent, new_rotary):
    spare = KEYS - LMAX - STEPS
    keys = jnp.concatenate([cache_latent, jnp.swapaxes(new_latent, 0, 1)], axis=1)
    keys = jnp.pad(keys, ((0, 0), (0, spare), (0, 0)))
    rotary_keys = jnp.concatenate([cache_rotary, jnp.transpose(new_rotary, (1, 2, 0))], axis=2)
    rotary_keys = jnp.pad(rotary_keys, ((0, 0), (0, 0), (0, spare)))
    return pl.pallas_call(
        attend_kernel,
        in_specs=[pl.BlockSpec(memory_space=pltpu.SMEM)]
        + [pl.BlockSpec(memory_space=pltpu.VMEM)] * 3,
        out_specs=pl.BlockSpec(memory_space=pltpu.VMEM),
        out_shape=jax.ShapeDtypeStruct((CHIPS, ROWS_DEV, HC * STEPS, LAT), jnp.bfloat16),
        compiler_params=pltpu.CompilerParams(vmem_limit_bytes=16 * 2**20),
    )(lengths, queries, keys, rotary_keys)


def per_device(
    query_plain,
    query_rotary,
    key_up,
    value_up,
    output_weight,
    cache_latent,
    cache_rotary,
    lengths,
    new_latent,
    new_rotary,
    residual,
    norm_gain,
    expert_ids,
    gate_weights,
    expert_gate,
    expert_up,
    expert_down,
):
    f32 = jnp.float32
    bf16 = jnp.bfloat16
    core = lax.axis_index("ep") % 2
    expert = lax.axis_index("dp") * lax.axis_size("ep") + lax.axis_index("ep")

    queries = jnp.concatenate([query_plain, query_rotary], axis=2)
    queries = queries.reshape(STEPS, CHIPS, 2, ROWS_DEV, 2 * (NOPE + ROPE))
    kept = lax.dynamic_index_in_dim(queries, core, axis=2, keepdims=False)
    given = lax.dynamic_index_in_dim(queries, 1 - core, axis=2, keepdims=False)
    given = other_core(given)
    key_map = jnp.concatenate([key_up, other_core(key_up)], axis=0)
    value_map = jnp.concatenate([value_up, other_core(value_up)], axis=0)
    out_map = jnp.concatenate([output_weight, other_core(output_weight)], axis=0)
    split = 2 * NOPE
    plain = jnp.stack([kept[..., :split], given[..., :split]], axis=3)
    plain = plain.reshape(STEPS, CHIPS, ROWS_DEV, HC, NOPE)
    rotary = jnp.stack([kept[..., split:], given[..., split:]], axis=3)
    rotary = rotary.reshape(STEPS, CHIPS, ROWS_DEV, HC, ROPE)
    absorbed = jnp.einsum("sclhn,hnd->clhsd", plain, key_map, preferred_element_type=f32)
    absorbed = absorbed.astype(bf16).reshape(CHIPS, ROWS_DEV, HC * STEPS, LAT)
    rotary = jnp.transpose(rotary, (1, 2, 3, 0, 4)).reshape(CHIPS, ROWS_DEV, HC * STEPS, ROPE)
    sent = exchange(jnp.concatenate([absorbed, rotary], axis=3))
    mixed = attend(sent, cache_latent, cache_rotary, lengths, new_latent, new_rotary)
    mixed = exchange(mixed).reshape(CHIPS, ROWS_DEV, HC, STEPS, LAT)
    values = jnp.einsum("clhsd,hdv->clshv", mixed, value_map, preferred_element_type=f32)
    values = values.astype(bf16).reshape(CHIPS * RS, HC * VHEAD)
    parts = jnp.dot(values, out_map, preferred_element_type=f32).astype(bf16)
    parts = exchange(parts.reshape(CHIPS, RS, D))
    attention = jnp.sum(parts.astype(f32), axis=0)
    hidden = jnp.swapaxes(residual, 0, 1).reshape(RS, D).astype(f32) + attention
    normed = (
        hidden * lax.rsqrt(jnp.mean(hidden * hidden, axis=-1, keepdims=True) + 1e-06) * norm_gain
    ).astype(bf16)

    pair = jnp.stack([expert, expert ^ 1])

    weights = [
        pltpu.with_memory_space_constraint(w, place)
        for w, place in (
            (expert_gate, pltpu.VMEM),
            (expert_up, pltpu.HBM),
            (expert_down, pltpu.HBM),
        )
    ]

    def experts(own, twin):
        return run_experts(own, other_core(twin), *weights)

    def work(pieces, after=()):
        own, twin, put, weight = pick(pair, pieces, after)
        own, twin = experts(own, twin)
        return own, spread(put, weight, own, other_core(twin))

    rows = jnp.concatenate([normed, routing(expert_ids, gate_weights)], axis=1)
    rows = plane_exchange(jnp.broadcast_to(rows[None], (16, RS, D + BESIDE)))
    rows = rows.reshape(BLOCK, D + BESIDE)
    half = BLOCK // 2
    low, high = rows[:half], rows[half:]
    before_low, after_high = shift(low, 0, 1), shift(high, 0, -1)
    before_high, after_low = shift(high, 0, 1), shift(low, 0, -1)
    far = [shift(before_low, 0, 1), shift(after_high, 0, -1)]

    here = mark(rows[:16, :128], weights[0])
    result, (first_low, first_high) = work([before_low, after_high], [here])
    result, (near_low, near_high) = work([after_low, before_high], [result])
    result, (far_low, far_high) = work(far, [result, first_low])
    first_low, first_high = shift(first_low, 0, -1), shift(first_high, 0, 1)
    far_low, far_high = shift(far_low, 0, 1), shift(far_high, 0, -1)
    near_low, near_high = shift(near_low + far_low, 0, 1), shift(near_high + far_high, 0, -1)
    _, (low, high) = work([rows], [result, first_low, first_high])
    total = [
        sum(x.astype(f32) for x in parts).astype(bf16)
        for parts in ((low, first_low, near_low), (high, first_high, near_high))
    ]
    total = jnp.concatenate(total, axis=0)
    routed = plane_exchange(total.reshape(16, RS, D))
    out = (hidden + jnp.sum(routed.astype(f32), axis=0)).astype(bf16)
    return jnp.swapaxes(out.reshape(ROWS_DEV, STEPS, D), 0, 1)


def solution(mesh):
    return jax.shard_map(
        per_device,
        mesh=mesh,
        in_specs=(
            P(None, "dp", "ep"),
            P(None, "dp", "ep"),
            P("ep", None, None),
            P("ep", None, None),
            P("ep", None),
            P(("dp", "ep"), None, None),
            P(("dp", "ep"), None, None),
            P(("dp", "ep")),
            P(None, ("dp", "ep"), None),
            P(None, ("dp", "ep"), None),
            P(None, ("dp", "ep"), None),
            P(),
            P(None, ("dp", "ep"), None),
            P(None, ("dp", "ep"), None),
            P(("dp", "ep"), None, None),
            P(("dp", "ep"), None, None),
            P(("dp", "ep"), None, None),
        ),
        out_specs=P(None, ("dp", "ep"), None),
        check_vma=False,
    )
```
